32 devices in a mesh: grp: 4 (over x, core), wav: 8 (over z, y).
Axes of the slice: x: 2, y: 2, z: 4, core: 2. Of those that a mesh axis runs over, the one named last changes fastest.
Arguments:
- spectra: float32 [3, 8, 16, 2, 2560], P(None, 'grp', 'wav'), may hold values from -6 to 6
- legendre: float32 [16, 2560, 32], P('wav'), may hold values from -0.03125 to 0.03125
- wave_number: int32 [16], replicated, may hold values from 0 to 2559, as said below
- cycle_points: int32 [32], replicated, may hold values from 20 to 10256, as said below
- cycle_owner: int32 [64], replicated, may hold values from 0 to 63, each once
Outputs:
- grid_columns: float32 [64, 3, 8, 11264], P('grp', None, None, 'wav')
The draws below stay inside these ranges and needn't reach their ends.
Inputs may be any that keep to these rules, and one draw needn't show every extreme that they name: `wave_number`: all distinct; entries 2 i and 2 i + 1 sum to 2559. `cycle_points`: each is 20 + 4 k for a whole k, rising with the latitude index; 20 and 10256 both occur. `cycle_owner`: A permutation of the cycles: 0 to 31 northern, 32 + i the southern mirror of latitude i.
All inputs are finite; a program needn't handle non-finite values.
Results may differ from the reference program's by a relative error of at most 0.0003.
Values sent between devices are 32-bit elements; how exact they have to be, the bound alone decides.
A program may use at most 128 MiB of HBM per device.

```python
import jax
import jax.numpy as jnp
from jax import lax

NTR = 2560
RMAX = 10256
MW = 16
NH = 32
NR = 64
LEV = 8
PAD = 11264


def draw_wave_number(key, part):
    half_count = MW // 2
    first_key, second_key = jax.random.split(jax.random.fold_in(key, 11))
    others = 1 + jax.random.permutation(first_key, NTR // 2 - 1)[:half_count - 1]
    lowest = jnp.concatenate([jnp.zeros((1,), jnp.int32), others.astype(jnp.int32)])
    lowest = lowest[jax.random.permutation(second_key, half_count)]
    paired = jnp.stack([lowest, NTR - 1 - lowest], axis=1).reshape(MW)
    return paired.astype(jnp.int32)


def draw_cycle_points(key, part):
    top_index = (RMAX - 20) // 4
    inner = 1 + jax.random.permutation(jax.random.fold_in(key, 23), top_index - 1)[:NH - 2]
    ends = jnp.array([0, top_index], dtype=jnp.int32)
    ordered = jnp.sort(jnp.concatenate([ends, inner.astype(jnp.int32)]))
    return (20 + 4 * ordered).astype(jnp.int32)


def shard_levels(stream_key, dims, shards, low, high):
    gain = 1.0
    for position, blocks in shards:
        steps = jax.random.uniform(jax.random.fold_in(jax.random.fold_in(stream_key, 6), position), (blocks,), jnp.float32, low / len(shards), high / len(shards))
        gain = gain * jnp.repeat(jnp.exp(steps), dims[position] // blocks).reshape((-1,) + (1,) * (len(dims) - 1 - position))
    return gain


def scatter_about(own_key, extent, spread, reach, cuts=(), kind=jnp.bfloat16):
    factor_of = shard_levels(own_key, extent, cuts, -0.22, 0.18) if cuts else 1.0
    values = jax.random.normal(own_key, extent, jnp.float32) * spread * factor_of
    return jnp.minimum(jnp.maximum(values, -reach), reach).astype(kind)


def setup_inputs(seed: int = 0) -> dict:
    key_of = jax.random.split(jax.random.key(seed), 6)
    spectra = scatter_about(key_of[0], (3, LEV, MW, 2, NTR), 1.0, 6.0, ((1, 4), (2, 8)), jnp.float32)
    legendre = scatter_about(key_of[1], (MW, NTR, NH), (NTR * MW) ** -0.5, 0.03125, ((0, 8),), jnp.float32)
    wave_number = draw_wave_number(jax.random.fold_in(key_of[5], 71), 0)
    cycle_points = draw_cycle_points(jax.random.fold_in(key_of[5], 71), 0)
    cycle_owner = jax.random.permutation(key_of[4], NR).astype(jnp.int32)
    return {"spectra": spectra, "legendre": legendre, "wave_number": wave_number, "cycle_points": cycle_points, "cycle_owner": cycle_owner}


TWO_PI = 6.283185307179586
HIGHEST = lax.Precision.HIGHEST


def synthesis(coeffs, wave_list, lengths, offset, points_count):
    points = offset + jnp.arange(points_count, dtype=jnp.int32)
    weight = jnp.where(wave_list == 0, 1.0, 2.0).astype(jnp.float32)
    wave_total = wave_list.shape[0]

    def one_cycle(cycle_args):
        cycle_block, cycle_length = cycle_args
        phases = (wave_list[:, None] * points[None, :]) % cycle_length
        angles = phases.astype(jnp.float32) * (TWO_PI / cycle_length.astype(jnp.float32))
        cosine = weight[:, None] * jnp.cos(angles)
        sine_part = -weight[:, None] * jnp.sin(angles)
        fourier_basis = jnp.stack([cosine, sine_part], axis=1).reshape(2 * wave_total, points_count)
        flattened = cycle_block.reshape(-1, 2 * wave_total)
        values = jnp.dot(flattened, fourier_basis, precision=HIGHEST, preferred_element_type=jnp.float32)
        values = jnp.where(points[None, :] < cycle_length, values, 0.0)
        return values.reshape(cycle_block.shape[:-1] + (points_count,))

    return lax.map(one_cycle, (coeffs, lengths))


def reference(spectra, legendre, wave_number, cycle_points, cycle_owner):
    offsets = jnp.arange(NTR, dtype=jnp.int32)
    inside = (wave_number[:, None] + offsets[None, :]) < NTR
    masked = jnp.where(inside[None, None, :, None, :], spectra, 0.0)
    parity_signs = jnp.where(offsets % 2 == 0, 1.0, -1.0).astype(jnp.float32)

    def one_wave(wave_args):
        coefficients, wave_table = wave_args
        mirrored = jnp.concatenate([wave_table, wave_table * parity_signs[:, None]], axis=1)
        return jnp.einsum("flck,kr->flcr", coefficients, mirrored, precision=HIGHEST)

    fourier = lax.map(one_wave, (jnp.moveaxis(masked, 2, 0), legendre))
    placed = jnp.take(fourier, cycle_owner, axis=4)
    rows_first = jnp.transpose(placed, (4, 1, 2, 0, 3)).reshape(NR, 3, LEV, 2 * MW)
    cycle_lengths = jnp.concatenate([cycle_points, cycle_points])[cycle_owner]
    return synthesis(rows_first, wave_number, cycle_lengths, 0, PAD)
```

```python
import functools
import math

import jax
import jax.numpy as jnp
from jax import lax
from jax.experimental import pallas as pl
from jax.experimental.pallas import tpu as pltpu
from jax.sharding import PartitionSpec as P

RMAX = 10256
SLOTS = 8
VMEM_BYTES = 48 * 2**20
MESH = pl.DeviceIdType.MESH


def iota(shape, dim):
    return lax.broadcasted_iota(jnp.int32, shape, dim)


def split(x):
    high = x.astype(jnp.bfloat16)
    return high, (x - high.astype(jnp.float32)).astype(jnp.bfloat16)


def dot(a, b, dims=((1,), (0,))):
    return lax.dot_general(a, b, (dims, ((), ())), preferred_element_type=jnp.float32)


def spread(groups, columns, spec, leg, wave, owner, out, rows, send, send_sem, recv_sem):
    devices = groups * columns
    g, w = lax.axis_index("grp"), lax.axis_index("wav")
    me = g * columns + w
    barrier = pltpu.get_barrier_semaphore()

    def place(step):
        other = lax.rem(me + step, devices)
        return lax.div(other, columns), lax.rem(other, columns)

    @pl.loop(1, devices)
    def _(step):
        pl.semaphore_signal(barrier, inc=1, device_id=place(step), device_id_type=MESH)

    fields, levels, waves, _, degrees = spec.shape
    half = leg.shape[2]
    lanes = send.shape[2]
    lane_row = iota((1, groups * lanes), 1) // SLOTS
    cycle = jnp.zeros((1, groups * lanes), jnp.int32)
    for row in range(2 * half):
        cycle = jnp.where(lane_row == row, owner[row], cycle)
    northern = iota((half, groups * lanes), 0)
    pick = [
        (northern + h * half == cycle).astype(jnp.float32).astype(jnp.bfloat16) for h in range(2)
    ]
    slot = iota((16, groups * lanes), 1) % SLOTS == iota((16, groups * lanes), 0) // 2
    degree = iota((16, degrees), 1)
    placed = []
    for q in range(waves):
        rows[q, 8:16, :] = jnp.zeros((8, degrees), jnp.float32)
        for f in range(fields):
            for l in range(levels):
                at = 2 * (f * levels + l)
                rows[q, at : at + 2, :] = spec[f, l, q]
        number = wave[w * waves + q]
        masked = jnp.where(degree + number < degrees, rows[q], 0.0)
        mirrored = jnp.where(degree % 2 == 0, masked, -masked)
        high, low = split(jnp.concatenate([masked, mirrored], axis=0))
        table_high, table_low = split(leg[q])
        both = dot(jnp.concatenate([high, low], axis=0), table_high)
        fourier = both[:32] + both[32:] + dot(high, table_low)
        total = jnp.zeros((16, groups * lanes), jnp.float32)
        for h in range(2):
            high, low = split(fourier[16 * h : 16 * h + 16])
            moved = dot(jnp.concatenate([high, low], axis=0), pick[h])
            total = total + moved[:16] + moved[16:]
        total = jnp.where(slot, total, 0.0)
        total = total[:8] + total[8:]
        total = total + pltpu.roll(total, 4, 0)
        placed.append(total + pltpu.roll(total, 2, 0))
    message = jnp.where(iota(placed[0].shape, 0) < 2, placed[0], placed[1])
    for to in range(groups):
        send[to] = message[:4, to * lanes : (to + 1) * lanes]
    out[g, w] = send[g]

    pl.semaphore_wait(barrier, devices - 1)

    def copy(step, source):
        to_g, to_w = place(step)
        from_g, from_w = source
        return pltpu.make_async_remote_copy(
            src_ref=send.at[to_g],
            dst_ref=out.at[from_g, from_w],
            send_sem=send_sem.at[to_g, to_w],
            recv_sem=recv_sem.at[from_g, from_w],
            device_id=(to_g, to_w),
            device_id_type=MESH,
        )

    @pl.loop(1, devices)
    def _(step):
        copy(step, (g, w)).start()

    @pl.loop(1, devices)
    def _(step):
        copy(step, place(step)).wait_recv()

    @pl.loop(1, devices)
    def _(step):
        copy(step, (g, w)).wait_send()


def reduced(x, length, inverse):
    turns = jnp.floor(x.astype(jnp.float32) * inverse).astype(jnp.int32)
    left = x - turns * length
    left = jnp.where(left < 0, left + length, left)
    return jnp.where(left >= length, left - length, left)


def cosine(x, length, inverse):
    left = reduced(x, length, inverse)
    left = jnp.where(2 * left > length, left - length, left)
    half = left.astype(jnp.float32) * (inverse * math.pi)
    square = half * half
    series = jnp.full_like(square, 1.0 / math.factorial(13))
    for power in (11, 9, 7, 5, 3, 1):
        sign = -1.0 if power % 4 == 3 else 1.0
        series = series * square + sign / math.factorial(power)
    sine = series * half
    return 1.0 - 2.0 * sine * sine


def synthesis(columns, got, wave, points, owner, out, coeffs, swapped, grid, out_sem):
    groups, lanes = got.shape[0], got.shape[3]
    depth = 4 * columns
    count, fields, level_total, segment = grid.shape
    levels = level_total // groups
    block = fields * level_total
    copies = -(-3 * depth // 128) * 128 // depth
    wide = copies * depth
    tiles = segment // 128
    tile_rows = -(-tiles // 8) * 8
    g, w = lax.axis_index("grp"), lax.axis_index("wav")

    x = jnp.concatenate([got[i].reshape(depth, lanes) for i in range(groups)], axis=1)
    even = iota(x.shape, 0) % 2 == 0
    partner = jnp.where(even, pltpu.roll(x, depth - 1, 0), pltpu.roll(x, 1, 0))
    target = iota((count * block, 1), 0)
    inner = lax.rem(target, block)
    level = lax.rem(inner, level_total)
    target = (
        lax.div(level, levels) * lanes
        + lax.div(target, block) * SLOTS
        + lax.div(inner, level_total) * levels
        + lax.rem(level, levels)
    )
    move = iota((count * block, groups * lanes), 1) == target
    move = move.astype(jnp.float32).astype(jnp.bfloat16)
    for values, ref in ((x, coeffs), (partner, swapped)):
        high, low = split(values)
        ref[...] = dot(move, jnp.concatenate([high] * copies, axis=0), ((1,), (1,))) + dot(
            move, jnp.concatenate([low] * copies, axis=0), ((1,), (1,))
        )

    deep = iota((depth, 128), 0)
    deep_wave = jnp.zeros((depth, 128), jnp.int32)
    across = iota((tile_rows, wide), 1) % depth
    across_wave = jnp.zeros((tile_rows, wide), jnp.int32)
    for q in range(depth // 2):
        deep_wave = jnp.where(deep // 2 == q, wave[q], deep_wave)
        across_wave = jnp.where(across // 2 == q, wave[q], across_wave)
    near = deep_wave * iota((depth, 128), 1)
    far = across_wave * (w * segment + 128 * iota((tile_rows, wide), 0))
    weight = jnp.where(across_wave == 0, 1.0, 2.0)
    rest = (iota((block * tiles, wide), 1) // depth) % 2 == 1
    point = iota((block, 128), 1) + w * segment

    def write(p):
        return pltpu.make_async_copy(grid.at[p], out.at[p], out_sem.at[p])

    @pl.loop(0, count, unroll=4)
    def _(p):
        length = points[lax.rem(owner[g * count + p], points.shape[0])]
        quarter = lax.div(length, 4)
        inverse = 1.0 / jnp.full((1, 128), length, jnp.int32).astype(jnp.float32)
        high, low = split(cosine(near + (deep % 2) * quarter, length, inverse))
        basis = jnp.concatenate([high, high, low, low][:copies], axis=0)
        inverse = jnp.concatenate([inverse] * (wide // 128), axis=1)
        turn = weight * cosine(far, length, inverse)
        cross = weight * cosine(far + (1 + 2 * (across % 2)) * quarter, length, inverse)
        start = pl.multiple_of(p * block, 8)
        own, other = coeffs[pl.ds(start, block), :], swapped[pl.ds(start, block), :]
        turned = jnp.concatenate(
            [own * turn[t : t + 1] + other * cross[t : t + 1] for t in range(tiles)], axis=0
        )
        head = turned.astype(jnp.bfloat16).astype(jnp.float32)
        parts = jnp.where(rest, turned - head, head).astype(jnp.bfloat16)
        values = dot(parts, basis)
        for t in range(tiles):
            kept = jnp.where(point + 128 * t < length, values[t * block : (t + 1) * block], 0.0)
            grid[p, :, :, 128 * t : 128 * (t + 1)] = kept.reshape(fields, level_total, 128)
        write(p).start()

    @pl.loop(0, count)
    def _(p):
        write(p).wait()


def body(groups, columns, spectra, legendre, wave_number, cycle_points, cycle_owner):
    fields, levels, waves, _, degrees = spectra.shape
    half = legendre.shape[2]
    count = 2 * half // groups
    lanes = count * SLOTS
    level_total = levels * groups
    segment = (RMAX + 128 * columns - 1) // (128 * columns) * 128
    vmem, smem = pl.BlockSpec(memory_space=pltpu.VMEM), pl.BlockSpec(memory_space=pltpu.SMEM)
    got = pl.pallas_call(
        functools.partial(spread, groups, columns),
        out_shape=jax.ShapeDtypeStruct((groups, columns, 4, lanes), jnp.float32),
        in_specs=[vmem, vmem, smem, smem],
        out_specs=vmem,
        scratch_shapes=[
            pltpu.VMEM((waves, 16, degrees), jnp.float32),
            pltpu.VMEM((groups, 4, lanes), jnp.float32),
            pltpu.SemaphoreType.DMA((groups, columns)),
            pltpu.SemaphoreType.DMA((groups, columns)),
        ],
        compiler_params=pltpu.CompilerParams(
            collective_id=0, has_side_effects=True, vmem_limit_bytes=VMEM_BYTES
        ),
        name="spread",
    )(spectra, legendre, wave_number, cycle_owner)
    wide = -(-3 * 4 * columns // 128) * 128
    block = fields * level_total
    return pl.pallas_call(
        functools.partial(synthesis, columns),
        out_shape=jax.ShapeDtypeStruct((count, fields, level_total, segment), jnp.float32),
        in_specs=[vmem, smem, smem, smem],
        out_specs=pl.BlockSpec(memory_space=pl.ANY),
        scratch_shapes=[
            pltpu.VMEM((count * block, wide), jnp.float32),
            pltpu.VMEM((count * block, wide), jnp.float32),
            pltpu.VMEM((count, fields, level_total, segment), jnp.float32),
            pltpu.SemaphoreType.DMA((count,)),
        ],
        compiler_params=pltpu.CompilerParams(vmem_limit_bytes=VMEM_BYTES),
        name="synthesis",
    )(got, wave_number, cycle_points, cycle_owner)


def solution(mesh):
    in_specs = (P(None, "grp", "wav", None, None), P("wav", None, None), P(), P(), P())
    out_specs = P("grp", None, None, "wav")
    groups, columns = mesh.shape["grp"], mesh.shape["wav"]
    return jax.shard_map(
        functools.partial(body, groups, columns),
        mesh=mesh,
        in_specs=in_specs,
        out_specs=out_specs,
        check_vma=False,
    )
```

```python
import functools
import math

import jax
import jax.numpy as jnp
from jax import lax
from jax.experimental import pallas as pl
from jax.experimental.pallas import tpu as pltpu
from jax.sharding import PartitionSpec as P

RMAX = 10256
SLOTS = 8
VMEM_BYTES = 48 * 2**20
MESH = pl.DeviceIdType.MESH


def iota(shape, dim):
    return lax.broadcasted_iota(jnp.int32, shape, dim)


def split(x):
    high = x.astype(jnp.bfloat16)
    return high, (x - high.astype(jnp.float32)).astype(jnp.bfloat16)


def dot(a, b, dims=((1,), (0,))):
    return lax.dot_general(a, b, (dims, ((), ())), preferred_element_type=jnp.float32)


def reduced(x, length, inverse):
    turns = jnp.floor(x.astype(jnp.float32) * inverse).astype(jnp.int32)
    left = x - turns * length
    left = jnp.where(left < 0, left + length, left)
    return jnp.where(left >= length, left - length, left)


def cosine(x, length, inverse):
    left = reduced(x, length, inverse)
    left = jnp.where(2 * left > length, left - length, left)
    half = left.astype(jnp.float32) * (inverse * math.pi)
    square = half * half
    series = jnp.full_like(square, 1.0 / math.factorial(13))
    for power in (11, 9, 7, 5, 3, 1):
        sign = -1.0 if power % 4 == 3 else 1.0
        series = series * square + sign / math.factorial(power)
    sine = series * half
    return 1.0 - 2.0 * sine * sine


def tables(groups, columns, level_total, segment, wave, points, owner, move, basis, turn, cross):
    count, wide = basis.shape[:2]
    lanes, depth, levels = count * SLOTS, 4 * columns, level_total // groups
    block, copies, tile_rows = move.shape[0] // count, wide // depth, turn.shape[1]
    g, w = lax.axis_index("grp"), lax.axis_index("wav")
    target = iota((count * block, 1), 0)
    inner = lax.rem(target, block)
    level = lax.rem(inner, level_total)
    target = (
        lax.div(level, levels) * lanes
        + lax.div(target, block) * SLOTS
        + lax.div(inner, level_total) * levels
        + lax.rem(level, levels)
    )
    chosen = iota((count * block, groups * lanes), 1) == target
    move[...] = chosen.astype(jnp.float32).astype(jnp.bfloat16)
    deep = iota((depth, 128), 0)
    deep_wave = jnp.zeros((depth, 128), jnp.int32)
    across = iota((tile_rows, wide), 1) % depth
    across_wave = jnp.zeros((tile_rows, wide), jnp.int32)
    for q in range(depth // 2):
        deep_wave = jnp.where(deep // 2 == q, wave[q], deep_wave)
        across_wave = jnp.where(across // 2 == q, wave[q], across_wave)
    near = deep_wave * iota((depth, 128), 1)
    far = across_wave * (w * segment + 128 * iota((tile_rows, wide), 0))
    weight = jnp.where(across_wave == 0, 1.0, 2.0)

    @pl.loop(0, count, unroll=4)
    def _(p):
        length = points[lax.rem(owner[g * count + p], points.shape[0])]
        quarter = lax.div(length, 4)
        inverse = 1.0 / jnp.full((1, 128), length, jnp.int32).astype(jnp.float32)
        high, low = split(cosine(near + (deep % 2) * quarter, length, inverse))
        basis[p] = jnp.concatenate([high, high, low, low][:copies], axis=0)
        inverse = jnp.concatenate([inverse] * (wide // 128), axis=1)
        turn[p] = weight * cosine(far, length, inverse)
        cross[p] = weight * cosine(far + (1 + 2 * (across % 2)) * quarter, length, inverse)


def spread(
    groups, columns, segment, spec_in, leg_in, wave, points, owner, out, move, basis, turn, cross, spec,
    leg, rows, send, send_sem, recv_sem, in_sem,
):
    devices = groups * columns
    g, w = lax.axis_index("grp"), lax.axis_index("wav")
    me = g * columns + w
    barrier = pltpu.get_barrier_semaphore()
    loads = [
        pltpu.make_async_copy(spec_in, spec, in_sem.at[0]),
        pltpu.make_async_copy(leg_in, leg, in_sem.at[1]),
    ]
    for load in loads:
        load.start()

    def place(step):
        other = lax.rem(me + step, devices)
        return lax.div(other, columns), lax.rem(other, columns)

    @pl.loop(1, devices)
    def _(step):
        pl.semaphore_signal(barrier, inc=1, device_id=place(step), device_id_type=MESH)

    fields, levels, waves, _, degrees = spec.shape
    half = leg.shape[1]
    lanes = send.shape[2]
    lane_row = iota((1, groups * lanes), 1) // SLOTS
    cycle = jnp.zeros((1, groups * lanes), jnp.int32)
    for row in range(2 * half):
        cycle = jnp.where(lane_row == row, owner[row], cycle)
    northern = iota((half, groups * lanes), 0)
    pick = [
        (northern + h * half == cycle).astype(jnp.float32).astype(jnp.bfloat16) for h in range(2)
    ]
    slot = iota((16, groups * lanes), 1) % SLOTS == iota((16, groups * lanes), 0) // 2
    degree = iota((16, degrees), 1)
    placed = []
    for load in loads:
        load.wait()
    for q in range(waves):
        rows[q, 8:16, :] = jnp.zeros((8, degrees), jnp.float32)
        for f in range(fields):
            for l in range(levels):
                at = 2 * (f * levels + l)
                rows[q, at : at + 2, :] = spec[f, l, q]
        number = wave[w * waves + q]
        masked = jnp.where(degree + number < degrees, rows[q], 0.0)
        mirrored = jnp.where(degree % 2 == 0, masked, -masked)
        high, low = split(jnp.concatenate([masked, mirrored], axis=0))
        table_high, table_low = split(leg[q])
        both = dot(jnp.concatenate([high, low], axis=0), table_high, ((1,), (1,)))
        fourier = both[:32] + both[32:] + dot(high, table_low, ((1,), (1,)))
        total = jnp.zeros((16, groups * lanes), jnp.float32)
        for h in range(2):
            high, low = split(fourier[16 * h : 16 * h + 16])
            moved = dot(jnp.concatenate([high, low], axis=0), pick[h])
            total = total + moved[:16] + moved[16:]
        total = jnp.where(slot, total, 0.0)
        total = total[:8] + total[8:]
        total = total + pltpu.roll(total, 4, 0)
        placed.append(total + pltpu.roll(total, 2, 0))
    message = jnp.where(iota(placed[0].shape, 0) < 2, placed[0], placed[1])
    for to in range(groups):
        send[to] = message[:4, to * lanes : (to + 1) * lanes]
    out[g, w] = send[g]

    pl.semaphore_wait(barrier, devices - 1)

    def copy(step, source):
        to_g, to_w = place(step)
        from_g, from_w = source
        return pltpu.make_async_remote_copy(
            src_ref=send.at[to_g],
            dst_ref=out.at[from_g, from_w],
            send_sem=send_sem.at[to_g, to_w],
            recv_sem=recv_sem.at[from_g, from_w],
            device_id=(to_g, to_w),
            device_id_type=MESH,
        )

    @pl.loop(1, devices)
    def _(step):
        copy(step, (g, w)).start()

    tables(groups, columns, levels * groups, segment, wave, points, owner, move, basis, turn, cross)

    @pl.loop(1, devices)
    def _(step):
        copy(step, place(step)).wait_recv()

    @pl.loop(1, devices)
    def _(step):
        copy(step, (g, w)).wait_send()


def synthesis(columns, got, move, basis, turn, cross, points, owner, out, coeffs, swapped, grid, out_sem):
    groups, lanes = got.shape[0], got.shape[3]
    depth = 4 * columns
    count, fields, level_total, segment = grid.shape
    levels = level_total // groups
    block = fields * level_total
    copies = -(-3 * depth // 128) * 128 // depth
    wide = copies * depth
    tiles = segment // 128
    g, w = lax.axis_index("grp"), lax.axis_index("wav")

    x = jnp.concatenate([got[i].reshape(depth, lanes) for i in range(groups)], axis=1)
    even = iota(x.shape, 0) % 2 == 0
    partner = jnp.where(even, pltpu.roll(x, depth - 1, 0), pltpu.roll(x, 1, 0))
    for values, ref in ((x, coeffs), (partner, swapped)):
        high, low = split(values)
        ref[...] = dot(move[...], jnp.concatenate([high] * copies, axis=0), ((1,), (1,))) + dot(
            move[...], jnp.concatenate([low] * copies, axis=0), ((1,), (1,))
        )

    rest = (iota((block * tiles, wide), 1) // depth) % 2 == 1
    point = iota((block, 128), 1) + w * segment

    def write(p):
        return pltpu.make_async_copy(grid.at[p], out.at[p], out_sem.at[p])

    @pl.loop(0, count, unroll=4)
    def _(p):
        length = points[lax.rem(owner[g * count + p], points.shape[0])]
        start = pl.multiple_of(p * block, 8)
        own, other = coeffs[pl.ds(start, block), :], swapped[pl.ds(start, block), :]
        turned = jnp.concatenate(
            [own * turn[p, t : t + 1] + other * cross[p, t : t + 1] for t in range(tiles)], axis=0
        )
        head = turned.astype(jnp.bfloat16).astype(jnp.float32)
        parts = jnp.where(rest, turned - head, head).astype(jnp.bfloat16)
        values = dot(parts, basis[p])
        for t in range(tiles):
            kept = jnp.where(point + 128 * t < length, values[t * block : (t + 1) * block], 0.0)
            grid[p, :, :, 128 * t : 128 * (t + 1)] = kept.reshape(fields, level_total, 128)
        write(p).start()

    @pl.loop(0, count)
    def _(p):
        write(p).wait()


def body(groups, columns, spectra, legendre, wave_number, cycle_points, cycle_owner):
    fields, levels, waves, _, degrees = spectra.shape
    half = legendre.shape[2]
    count = 2 * half // groups
    lanes = count * SLOTS
    level_total = levels * groups
    segment = (RMAX + 128 * columns - 1) // (128 * columns) * 128
    vmem, smem = pl.BlockSpec(memory_space=pltpu.VMEM), pl.BlockSpec(memory_space=pltpu.SMEM)
    wide = -(-3 * 4 * columns // 128) * 128
    block = fields * level_total
    angles = jax.ShapeDtypeStruct((count, -(-segment // 1024) * 8, wide), jnp.float32)
    got, *angles = pl.pallas_call(
        functools.partial(spread, groups, columns, segment),
        out_shape=(
            jax.ShapeDtypeStruct((groups, columns, 4, lanes), jnp.float32),
            jax.ShapeDtypeStruct((count * block, groups * lanes), jnp.bfloat16),
            jax.ShapeDtypeStruct((count, wide, 128), jnp.bfloat16),
            angles,
            angles,
        ),
        in_specs=[pl.BlockSpec(memory_space=pltpu.HBM)] * 2 + [smem] * 3,
        out_specs=(vmem,) * 5,
        scratch_shapes=[
            pltpu.VMEM(spectra.shape, jnp.float32),
            pltpu.VMEM((waves, half, degrees), jnp.float32),
            pltpu.VMEM((waves, 16, degrees), jnp.float32),
            pltpu.VMEM((groups, 4, lanes), jnp.float32),
            pltpu.SemaphoreType.DMA((groups, columns)),
            pltpu.SemaphoreType.DMA((groups, columns)),
            pltpu.SemaphoreType.DMA((2,)),
        ],
        compiler_params=pltpu.CompilerParams(
            collective_id=0, has_side_effects=True, vmem_limit_bytes=VMEM_BYTES
        ),
        name="spread",
    )(spectra, jnp.swapaxes(legendre, 1, 2), wave_number, cycle_points, cycle_owner)
    return pl.pallas_call(
        functools.partial(synthesis, columns),
        out_shape=jax.ShapeDtypeStruct((count, fields, level_total, segment), jnp.float32),
        in_specs=[vmem] * 5 + [smem] * 2,
        out_specs=pl.BlockSpec(memory_space=pl.ANY),
        scratch_shapes=[
            pltpu.VMEM((count * block, wide), jnp.float32),
            pltpu.VMEM((count * block, wide), jnp.float32),
            pltpu.VMEM((count, fields, level_total, segment), jnp.float32),
            pltpu.SemaphoreType.DMA((count,)),
        ],
        compiler_params=pltpu.CompilerParams(vmem_limit_bytes=VMEM_BYTES),
        name="synthesis",
    )(got, *angles, cycle_points, cycle_owner)


def solution(mesh):
    in_specs = (P(None, "grp", "wav", None, None), P("wav", None, None), P(), P(), P())
    out_specs = P("grp", None, None, "wav")
    groups, columns = mesh.shape["grp"], mesh.shape["wav"]
    return jax.shard_map(
        functools.partial(body, groups, columns),
        mesh=mesh,
        in_specs=in_specs,
        out_specs=out_specs,
        check_vma=False,
    )
```

```python
import functools
import math

import jax
import jax.numpy as jnp
from jax import lax
from jax.experimental import pallas as pl
from jax.experimental.pallas import tpu as pltpu
from jax.sharding import PartitionSpec as P

RMAX = 10256
SLOTS = 8
VMEM_BYTES = 65000 * 2**10
MESH = pl.DeviceIdType.MESH


def iota(shape, dim):
    return lax.broadcasted_iota(jnp.int32, shape, dim)


def split(x):
    high = x.astype(jnp.bfloat16)
    return high, (x - high.astype(jnp.float32)).astype(jnp.bfloat16)


def dot(a, b, dims=((1,), (0,))):
    return lax.dot_general(a, b, (dims, ((), ())), preferred_element_type=jnp.float32)


def spread(groups, columns, spec_in, leg_in, wave, owner, out, spec, leg, rows, send, send_sem, recv_sem, in_sem):
    devices = groups * columns
    g, w = lax.axis_index("grp"), lax.axis_index("wav")
    me = g * columns + w
    barrier = pltpu.get_barrier_semaphore()
    loads = [
        pltpu.make_async_copy(spec_in, spec, in_sem.at[0]),
        pltpu.make_async_copy(leg_in, leg, in_sem.at[1]),
    ]
    for load in loads:
        load.start()

    def place(step):
        other = lax.rem(me + step, devices)
        return lax.div(other, columns), lax.rem(other, columns)

    @pl.loop(1, devices)
    def _(step):
        pl.semaphore_signal(barrier, inc=1, device_id=place(step), device_id_type=MESH)

    fields, levels, waves, _, degrees = spec.shape
    half = leg.shape[1]
    lanes = send.shape[2]
    lane_row = iota((1, groups * lanes), 1) // SLOTS
    cycle = jnp.zeros((1, groups * lanes), jnp.int32)
    for row in range(2 * half):
        cycle = jnp.where(lane_row == row, owner[row], cycle)
    northern = iota((half, groups * lanes), 0)
    pick = [
        (northern + h * half == cycle).astype(jnp.float32).astype(jnp.bfloat16) for h in range(2)
    ]
    slot = iota((16, groups * lanes), 1) % SLOTS == iota((16, groups * lanes), 0) // 2
    degree = iota((16, degrees), 1)
    placed = []
    for load in loads:
        load.wait()
    for q in range(waves):
        rows[q, 8:16, :] = jnp.zeros((8, degrees), jnp.float32)
        for f in range(fields):
            for l in range(levels):
                at = 2 * (f * levels + l)
                rows[q, at : at + 2, :] = spec[f, l, q]
        number = wave[w * waves + q]
        masked = jnp.where(degree + number < degrees, rows[q], 0.0)
        mirrored = jnp.where(degree % 2 == 0, masked, -masked)
        high, low = split(jnp.concatenate([masked, mirrored], axis=0))
        table_high, table_low = split(leg[q])
        both = dot(jnp.concatenate([high, low], axis=0), table_high, ((1,), (1,)))
        fourier = both[:32] + both[32:] + dot(high, table_low, ((1,), (1,)))
        total = jnp.zeros((16, groups * lanes), jnp.float32)
        for h in range(2):
            high, low = split(fourier[16 * h : 16 * h + 16])
            moved = dot(jnp.concatenate([high, low], axis=0), pick[h])
            total = total + moved[:16] + moved[16:]
        total = jnp.where(slot, total, 0.0)
        total = total[:8] + total[8:]
        total = total + pltpu.roll(total, 4, 0)
        placed.append(total + pltpu.roll(total, 2, 0))
    message = jnp.where(iota(placed[0].shape, 0) < 2, placed[0], placed[1])
    for to in range(groups):
        send[to] = message[:4, to * lanes : (to + 1) * lanes]
    out[g, w] = send[g]

    pl.semaphore_wait(barrier, devices - 1)

    def copy(step, source):
        to_g, to_w = place(step)
        from_g, from_w = source
        return pltpu.make_async_remote_copy(
            src_ref=send.at[to_g],
            dst_ref=out.at[from_g, from_w],
            send_sem=send_sem.at[to_g, to_w],
            recv_sem=recv_sem.at[from_g, from_w],
            device_id=(to_g, to_w),
            device_id_type=MESH,
        )

    @pl.loop(1, devices)
    def _(step):
        copy(step, (g, w)).start()

    @pl.loop(1, devices)
    def _(step):
        copy(step, place(step)).wait_recv()

    @pl.loop(1, devices)
    def _(step):
        copy(step, (g, w)).wait_send()


def reduced(x, length, inverse):
    turns = jnp.floor(x.astype(jnp.float32) * inverse).astype(jnp.int32)
    left = x - turns * length
    left = jnp.where(left < 0, left + length, left)
    return jnp.where(left >= length, left - length, left)


def cosine(x, length, inverse):
    left = reduced(x, length, inverse)
    left = jnp.where(2 * left > length, left - length, left)
    half = left.astype(jnp.float32) * (inverse * math.pi)
    square = half * half
    series = jnp.full_like(square, 1.0 / math.factorial(13))
    for power in (11, 9, 7, 5, 3, 1):
        sign = -1.0 if power % 4 == 3 else 1.0
        series = series * square + sign / math.factorial(power)
    sine = series * half
    return 1.0 - 2.0 * sine * sine


def synthesis(columns, got, wave, points, owner, out, coeffs, swapped, grid, out_sem):
    groups, lanes = got.shape[0], got.shape[3]
    depth = 4 * columns
    count, fields, level_total, segment = grid.shape
    levels = level_total // groups
    block = fields * level_total
    copies = -(-3 * depth // 128) * 128 // depth
    wide = copies * depth
    tiles = segment // 128
    tile_rows = -(-tiles // 8) * 8
    g, w = lax.axis_index("grp"), lax.axis_index("wav")

    x = jnp.concatenate([got[i].reshape(depth, lanes) for i in range(groups)], axis=1)
    even = iota(x.shape, 0) % 2 == 0
    partner = jnp.where(even, pltpu.roll(x, depth - 1, 0), pltpu.roll(x, 1, 0))
    target = iota((count * block, 1), 0)
    inner = lax.rem(target, block)
    level = lax.rem(inner, level_total)
    target = (
        lax.div(level, levels) * lanes
        + lax.div(target, block) * SLOTS
        + lax.div(inner, level_total) * levels
        + lax.rem(level, levels)
    )
    move = iota((count * block, groups * lanes), 1) == target
    move = move.astype(jnp.float32).astype(jnp.bfloat16)
    for values, ref in ((x, coeffs), (partner, swapped)):
        high, low = split(values)
        ref[...] = dot(move, jnp.concatenate([high] * copies, axis=0), ((1,), (1,))) + dot(
            move, jnp.concatenate([low] * copies, axis=0), ((1,), (1,))
        )

    deep = iota((depth, 128), 0)
    deep_wave = jnp.zeros((depth, 128), jnp.int32)
    across = iota((tile_rows, wide), 1) % depth
    across_wave = jnp.zeros((tile_rows, wide), jnp.int32)
    for q in range(depth // 2):
        deep_wave = jnp.where(deep // 2 == q, wave[q], deep_wave)
        across_wave = jnp.where(across // 2 == q, wave[q], across_wave)
    near = deep_wave * iota((depth, 128), 1)
    far = across_wave * (w * segment + 128 * iota((tile_rows, wide), 0))
    weight = jnp.where(across_wave == 0, 1.0, 2.0)
    rest = (iota((block * tiles, wide), 1) // depth) % 2 == 1
    point = iota((block, 128), 1) + w * segment

    def write(p):
        return pltpu.make_async_copy(grid.at[p], out.at[p], out_sem.at[p])

    @pl.loop(0, count, unroll=4)
    def _(p):
        length = points[lax.rem(owner[g * count + p], points.shape[0])]
        quarter = lax.div(length, 4)
        inverse = 1.0 / jnp.full((1, 128), length, jnp.int32).astype(jnp.float32)
        high, low = split(cosine(near + (deep % 2) * quarter, length, inverse))
        basis = jnp.concatenate([high, high, low, low][:copies], axis=0)
        inverse = jnp.concatenate([inverse] * (wide // 128), axis=1)
        turn = weight * cosine(far, length, inverse)
        cross = weight * cosine(far + (1 + 2 * (across % 2)) * quarter, length, inverse)
        start = pl.multiple_of(p * block, 8)
        own, other = coeffs[pl.ds(start, block), :], swapped[pl.ds(start, block), :]
        turned = jnp.concatenate(
            [own * turn[t : t + 1] + other * cross[t : t + 1] for t in range(tiles)], axis=0
        )
        head = turned.astype(jnp.bfloat16).astype(jnp.float32)
        parts = jnp.where(rest, turned - head, head).astype(jnp.bfloat16)
        values = dot(parts, basis)
        for t in range(tiles):
            kept = jnp.where(point + 128 * t < length, values[t * block : (t + 1) * block], 0.0)
            grid[p, :, :, 128 * t : 128 * (t + 1)] = kept.reshape(fields, level_total, 128)
        write(p).start()

    @pl.loop(0, count)
    def _(p):
        write(p).wait()


def body(groups, columns, spectra, legendre, wave_number, cycle_points, cycle_owner):
    fields, levels, waves, _, degrees = spectra.shape
    half = legendre.shape[2]
    count = 2 * half // groups
    lanes = count * SLOTS
    level_total = levels * groups
    segment = (RMAX + 128 * columns - 1) // (128 * columns) * 128
    vmem, smem = pl.BlockSpec(memory_space=pltpu.VMEM), pl.BlockSpec(memory_space=pltpu.SMEM)
    got = pl.pallas_call(
        functools.partial(spread, groups, columns),
        out_shape=jax.ShapeDtypeStruct((groups, columns, 4, lanes), jnp.float32),
        in_specs=[pl.BlockSpec(memory_space=pltpu.HBM)] * 2 + [smem, smem],
        out_specs=vmem,
        scratch_shapes=[
            pltpu.VMEM(spectra.shape, jnp.float32),
            pltpu.VMEM((waves, half, degrees), jnp.float32),
            pltpu.VMEM((waves, 16, degrees), jnp.float32),
            pltpu.VMEM((groups, 4, lanes), jnp.float32),
            pltpu.SemaphoreType.DMA((groups, columns)),
            pltpu.SemaphoreType.DMA((groups, columns)),
            pltpu.SemaphoreType.DMA((2,)),
        ],
        compiler_params=pltpu.CompilerParams(
            collective_id=0, has_side_effects=True, vmem_limit_bytes=VMEM_BYTES
        ),
        name="spread",
    )(spectra, jnp.swapaxes(legendre, 1, 2), wave_number, cycle_owner)
    wide = -(-3 * 4 * columns // 128) * 128
    block = fields * level_total
    return pl.pallas_call(
        functools.partial(synthesis, columns),
        out_shape=jax.ShapeDtypeStruct((count, fields, level_total, segment), jnp.float32),
        in_specs=[vmem, smem, smem, smem],
        out_specs=pl.BlockSpec(memory_space=pl.ANY),
        scratch_shapes=[
            pltpu.VMEM((count * block, wide), jnp.float32),
            pltpu.VMEM((count * block, wide), jnp.float32),
            pltpu.VMEM((count, fields, level_total, segment), jnp.float32),
            pltpu.SemaphoreType.DMA((count,)),
        ],
        compiler_params=pltpu.CompilerParams(vmem_limit_bytes=VMEM_BYTES),
        name="synthesis",
    )(got, wave_number, cycle_points, cycle_owner)


def solution(mesh):
    in_specs = (P(None, "grp", "wav", None, None), P("wav", None, None), P(), P(), P())
    out_specs = P("grp", None, None, "wav")
    groups, columns = mesh.shape["grp"], mesh.shape["wav"]
    return jax.shard_map(
        functools.partial(body, groups, columns),
        mesh=mesh,
        in_specs=in_specs,
        out_specs=out_specs,
        check_vma=False,
    )
```

```python
import functools
import math

import jax
import jax.numpy as jnp
from jax import lax
from jax.experimental import pallas as pl
from jax.experimental.pallas import tpu as pltpu
from jax.sharding import PartitionSpec as P

RMAX = 10256
SLOTS = 8
VMEM_BYTES = 65000 * 2**10
MESH = pl.DeviceIdType.MESH


def iota(shape, dim):
    return lax.broadcasted_iota(jnp.int32, shape, dim)


def split(x):
    high = x.astype(jnp.bfloat16)
    return high, (x - high.astype(jnp.float32)).astype(jnp.bfloat16)


def dot(a, b, dims=((1,), (0,))):
    return lax.dot_general(a, b, (dims, ((), ())), preferred_element_type=jnp.float32)


def spread(groups, columns, spec_in, leg_in, wave, owner, out, spec, leg, rows, send, send_sem, recv_sem, in_sem):
    devices = groups * columns
    g, w = lax.axis_index("grp"), lax.axis_index("wav")
    barrier = pltpu.get_barrier_semaphore()
    loads = [
        pltpu.make_async_copy(spec_in, spec, in_sem.at[0]),
        pltpu.make_async_copy(leg_in, leg, in_sem.at[1]),
    ]
    for load in loads:
        load.start()

    def each(act):
        for over in range(groups):

            @pl.loop(1 if over == 0 else 0, columns, unroll=columns if columns <= 8 and over else 1)
            def _(along):
                act(lax.rem(g + over, groups), lax.rem(w + along, columns))

    each(lambda *to: pl.semaphore_signal(barrier, inc=1, device_id=to, device_id_type=MESH))

    fields, levels, waves, _, degrees = spec.shape
    half = leg.shape[1]
    lanes = send.shape[2]
    lane_row = iota((1, groups * lanes), 1) // SLOTS
    cycle = jnp.zeros((1, groups * lanes), jnp.int32)
    for row in range(2 * half):
        cycle = jnp.where(lane_row == row, owner[row], cycle)
    northern = iota((half, groups * lanes), 0)
    pick = [
        (northern + h * half == cycle).astype(jnp.float32).astype(jnp.bfloat16) for h in range(2)
    ]
    slot = iota((16, groups * lanes), 1) % SLOTS == iota((16, groups * lanes), 0) // 2
    degree = iota((16, degrees), 1)
    placed = []
    for load in loads:
        load.wait()
    for q in range(waves):
        rows[q, 8:16, :] = jnp.zeros((8, degrees), jnp.float32)
        for f in range(fields):
            for l in range(levels):
                at = 2 * (f * levels + l)
                rows[q, at : at + 2, :] = spec[f, l, q]
        number = wave[w * waves + q]
        masked = jnp.where(degree + number < degrees, rows[q], 0.0)
        mirrored = jnp.where(degree % 2 == 0, masked, -masked)
        high, low = split(jnp.concatenate([masked, mirrored], axis=0))
        table_high, table_low = split(leg[q])
        both = dot(jnp.concatenate([high, low], axis=0), table_high, ((1,), (1,)))
        fourier = both[:32] + both[32:] + dot(high, table_low, ((1,), (1,)))
        total = jnp.zeros((16, groups * lanes), jnp.float32)
        for h in range(2):
            high, low = split(fourier[16 * h : 16 * h + 16])
            moved = dot(jnp.concatenate([high, low], axis=0), pick[h])
            total = total + moved[:16] + moved[16:]
        total = jnp.where(slot, total, 0.0)
        total = total[:8] + total[8:]
        total = total + pltpu.roll(total, 4, 0)
        placed.append(total + pltpu.roll(total, 2, 0))
    message = jnp.where(iota(placed[0].shape, 0) < 2, placed[0], placed[1])
    for to in range(groups):
        send[to] = message[:4, to * lanes : (to + 1) * lanes]
    out[g, w] = send[g]

    pl.semaphore_wait(barrier, devices - 1)

    def copy(to, source):
        return pltpu.make_async_remote_copy(
            src_ref=send.at[to[0]],
            dst_ref=out.at[source[0], source[1]],
            send_sem=send_sem.at[to[0], to[1]],
            recv_sem=recv_sem.at[source[0], source[1]],
            device_id=to,
            device_id_type=MESH,
        )

    each(lambda *to: copy(to, (g, w)).start())
    each(lambda *source: copy(source, source).wait_recv())
    each(lambda *to: copy(to, (g, w)).wait_send())


def reduced(x, length, inverse):
    turns = jnp.floor(x.astype(jnp.float32) * inverse).astype(jnp.int32)
    left = x - turns * length
    left = jnp.where(left < 0, left + length, left)
    return jnp.where(left >= length, left - length, left)


def cosine(x, length, inverse):
    left = reduced(x, length, inverse)
    left = jnp.where(2 * left > length, left - length, left)
    half = left.astype(jnp.float32) * (inverse * math.pi)
    square = half * half
    series = jnp.full_like(square, 1.0 / math.factorial(13))
    for power in (11, 9, 7, 5, 3, 1):
        sign = -1.0 if power % 4 == 3 else 1.0
        series = series * square + sign / math.factorial(power)
    sine = series * half
    return 1.0 - 2.0 * sine * sine


def synthesis(columns, got, wave, points, owner, out, coeffs, swapped, grid, out_sem):
    groups, lanes = got.shape[0], got.shape[3]
    depth = 4 * columns
    count, fields, level_total, segment = grid.shape
    levels = level_total // groups
    block = fields * level_total
    copies = -(-3 * depth // 128) * 128 // depth
    wide = copies * depth
    tiles = segment // 128
    tile_rows = -(-tiles // 8) * 8
    g, w = lax.axis_index("grp"), lax.axis_index("wav")

    x = jnp.concatenate([got[i].reshape(depth, lanes) for i in range(groups)], axis=1)
    even = iota(x.shape, 0) % 2 == 0
    partner = jnp.where(even, pltpu.roll(x, depth - 1, 0), pltpu.roll(x, 1, 0))
    target = iota((count * block, 1), 0)
    inner = lax.rem(target, block)
    level = lax.rem(inner, level_total)
    target = (
        lax.div(level, levels) * lanes
        + lax.div(target, block) * SLOTS
        + lax.div(inner, level_total) * levels
        + lax.rem(level, levels)
    )
    move = iota((count * block, groups * lanes), 1) == target
    move = move.astype(jnp.float32).astype(jnp.bfloat16)
    for values, ref in ((x, coeffs), (partner, swapped)):
        high, low = split(values)
        ref[...] = dot(move, jnp.concatenate([high] * copies, axis=0), ((1,), (1,))) + dot(
            move, jnp.concatenate([low] * copies, axis=0), ((1,), (1,))
        )

    deep = iota((depth, 128), 0)
    deep_wave = jnp.zeros((depth, 128), jnp.int32)
    across = iota((tile_rows, wide), 1) % depth
    across_wave = jnp.zeros((tile_rows, wide), jnp.int32)
    for q in range(depth // 2):
        deep_wave = jnp.where(deep // 2 == q, wave[q], deep_wave)
        across_wave = jnp.where(across // 2 == q, wave[q], across_wave)
    near = deep_wave * iota((depth, 128), 1)
    far = across_wave * (w * segment + 128 * iota((tile_rows, wide), 0))
    weight = jnp.where(across_wave == 0, 1.0, 2.0)
    rest = (iota((block * tiles, wide), 1) // depth) % 2 == 1
    point = iota((block, 128), 1) + w * segment

    def write(p):
        return pltpu.make_async_copy(grid.at[p], out.at[p], out_sem.at[p])

    @pl.loop(0, count, unroll=8)
    def _(p):
        length = points[lax.rem(owner[g * count + p], points.shape[0])]
        quarter = lax.div(length, 4)
        inverse = 1.0 / jnp.full((1, 128), length, jnp.int32).astype(jnp.float32)
        high, low = split(cosine(near + (deep % 2) * quarter, length, inverse))
        basis = jnp.concatenate([high, high, low, low][:copies], axis=0)
        inverse = jnp.concatenate([inverse] * (wide // 128), axis=1)
        turn = weight * cosine(far, length, inverse)
        cross = weight * cosine(far + (1 + 2 * (across % 2)) * quarter, length, inverse)
        start = pl.multiple_of(p * block, 8)
        own, other = coeffs[pl.ds(start, block), :], swapped[pl.ds(start, block), :]
        turned = jnp.concatenate(
            [own * turn[t : t + 1] + other * cross[t : t + 1] for t in range(tiles)], axis=0
        )
        head = turned.astype(jnp.bfloat16).astype(jnp.float32)
        parts = jnp.where(rest, turned - head, head).astype(jnp.bfloat16)
        values = dot(parts, basis)
        for t in range(tiles):
            kept = jnp.where(point + 128 * t < length, values[t * block : (t + 1) * block], 0.0)
            grid[p, :, :, 128 * t : 128 * (t + 1)] = kept.reshape(fields, level_total, 128)
        write(p).start()

    @pl.loop(0, count)
    def _(p):
        write(p).wait()


def body(groups, columns, spectra, legendre, wave_number, cycle_points, cycle_owner):
    fields, levels, waves, _, degrees = spectra.shape
    half = legendre.shape[2]
    count = 2 * half // groups
    lanes = count * SLOTS
    level_total = levels * groups
    segment = (RMAX + 128 * columns - 1) // (128 * columns) * 128
    vmem, smem = pl.BlockSpec(memory_space=pltpu.VMEM), pl.BlockSpec(memory_space=pltpu.SMEM)
    got = pl.pallas_call(
        functools.partial(spread, groups, columns),
        out_shape=jax.ShapeDtypeStruct((groups, columns, 4, lanes), jnp.float32),
        in_specs=[pl.BlockSpec(memory_space=pltpu.HBM)] * 2 + [smem, smem],
        out_specs=vmem,
        scratch_shapes=[
            pltpu.VMEM(spectra.shape, jnp.float32),
            pltpu.VMEM((waves, half, degrees), jnp.float32),
            pltpu.VMEM((waves, 16, degrees), jnp.float32),
            pltpu.VMEM((groups, 4, lanes), jnp.float32),
            pltpu.SemaphoreType.DMA((groups, columns)),
            pltpu.SemaphoreType.DMA((groups, columns)),
            pltpu.SemaphoreType.DMA((2,)),
        ],
        compiler_params=pltpu.CompilerParams(
            collective_id=0, has_side_effects=True, vmem_limit_bytes=VMEM_BYTES
        ),
        name="spread",
    )(spectra, jnp.swapaxes(legendre, 1, 2), wave_number, cycle_owner)
    wide = -(-3 * 4 * columns // 128) * 128
    block = fields * level_total
    return pl.pallas_call(
        functools.partial(synthesis, columns),
        out_shape=jax.ShapeDtypeStruct((count, fields, level_total, segment), jnp.float32),
        in_specs=[vmem, smem, smem, smem],
        out_specs=pl.BlockSpec(memory_space=pl.ANY),
        scratch_shapes=[
            pltpu.VMEM((count * block, wide), jnp.float32),
            pltpu.VMEM((count * block, wide), jnp.float32),
            pltpu.VMEM((count, fields, level_total, segment), jnp.float32),
            pltpu.SemaphoreType.DMA((count,)),
        ],
        compiler_params=pltpu.CompilerParams(vmem_limit_bytes=VMEM_BYTES),
        name="synthesis",
    )(got, wave_number, cycle_points, cycle_owner)


def solution(mesh):
    in_specs = (P(None, "grp", "wav", None, None), P("wav", None, None), P(), P(), P())
    out_specs = P("grp", None, None, "wav")
    groups, columns = mesh.shape["grp"], mesh.shape["wav"]
    return jax.shard_map(
        functools.partial(body, groups, columns),
        mesh=mesh,
        in_specs=in_specs,
        out_specs=out_specs,
        check_vma=False,
    )
```

```python
import functools
import math

import jax
import jax.numpy as jnp
from jax import lax
from jax.experimental import pallas as pl
from jax.experimental.pallas import tpu as pltpu
from jax.sharding import PartitionSpec as P

RMAX = 10256
SLOTS = 8
VMEM_BYTES = 65000 * 2**10
MESH = pl.DeviceIdType.MESH


def iota(shape, dim):
    return lax.broadcasted_iota(jnp.int32, shape, dim)


def split(x):
    high = x.astype(jnp.bfloat16)
    return high, (x - high.astype(jnp.float32)).astype(jnp.bfloat16)


def dot(a, b, dims=((1,), (0,))):
    return lax.dot_general(a, b, (dims, ((), ())), preferred_element_type=jnp.float32)


def spread(groups, columns, spec_in, leg_in, wave, owner, out, spec, leg, rows, send, send_sem, recv_sem, in_sem):
    devices = groups * columns
    g, w = lax.axis_index("grp"), lax.axis_index("wav")
    barrier = pltpu.get_barrier_semaphore()
    loads = [
        pltpu.make_async_copy(spec_in, spec, in_sem.at[0]),
        pltpu.make_async_copy(leg_in, leg, in_sem.at[1]),
    ]
    for load in loads:
        load.start()

    def each(act):
        for over in range(groups):

            @pl.loop(1 if over == 0 else 0, columns, unroll=columns - (over == 0) if columns <= 8 else 1)
            def _(along):
                act(lax.rem(g + over, groups), lax.rem(w + along, columns))

    each(lambda *to: pl.semaphore_signal(barrier, inc=1, device_id=to, device_id_type=MESH))

    fields, levels, waves, _, degrees = spec.shape
    half = leg.shape[1]
    lanes = send.shape[2]
    lane_row = iota((1, groups * lanes), 1) // SLOTS
    cycle = jnp.zeros((1, groups * lanes), jnp.int32)
    for row in range(2 * half):
        cycle = jnp.where(lane_row == row, owner[row], cycle)
    northern = iota((half, groups * lanes), 0)
    pick = [
        (northern + h * half == cycle).astype(jnp.float32).astype(jnp.bfloat16) for h in range(2)
    ]
    slot = iota((16, groups * lanes), 1) % SLOTS == iota((16, groups * lanes), 0) // 2
    degree = iota((16, degrees), 1)
    placed = []
    for load in loads:
        load.wait()
    for q in range(waves):
        rows[q, 8:16, :] = jnp.zeros((8, degrees), jnp.float32)
        for f in range(fields):
            for l in range(levels):
                at = 2 * (f * levels + l)
                rows[q, at : at + 2, :] = spec[f, l, q]
        number = wave[w * waves + q]
        masked = jnp.where(degree + number < degrees, rows[q], 0.0)
        mirrored = jnp.where(degree % 2 == 0, masked, -masked)
        high, low = split(jnp.concatenate([masked, mirrored], axis=0))
        table_high, table_low = split(leg[q])
        both = dot(jnp.concatenate([high, low], axis=0), table_high, ((1,), (1,)))
        fourier = both[:32] + both[32:] + dot(high, table_low, ((1,), (1,)))
        total = jnp.zeros((16, groups * lanes), jnp.float32)
        for h in range(2):
            high, low = split(fourier[16 * h : 16 * h + 16])
            moved = dot(jnp.concatenate([high, low], axis=0), pick[h])
            total = total + moved[:16] + moved[16:]
        total = jnp.where(slot, total, 0.0)
        total = total[:8] + total[8:]
        total = total + pltpu.roll(total, 4, 0)
        placed.append(total + pltpu.roll(total, 2, 0))
    message = jnp.where(iota(placed[0].shape, 0) < 2, placed[0], placed[1])
    for to in range(groups):
        send[to] = message[:4, to * lanes : (to + 1) * lanes]
    out[g, w] = send[g]

    pl.semaphore_wait(barrier, devices - 1)

    def copy(to, source):
        return pltpu.make_async_remote_copy(
            src_ref=send.at[to[0]],
            dst_ref=out.at[source[0], source[1]],
            send_sem=send_sem.at[to[0], to[1]],
            recv_sem=recv_sem.at[source[0], source[1]],
            device_id=to,
            device_id_type=MESH,
        )

    each(lambda *to: copy(to, (g, w)).start())
    each(lambda *source: copy(source, source).wait_recv())
    each(lambda *to: copy(to, (g, w)).wait_send())


def reduced(x, length, inverse):
    turns = jnp.floor(x.astype(jnp.float32) * inverse).astype(jnp.int32)
    left = x - turns * length
    left = jnp.where(left < 0, left + length, left)
    return jnp.where(left >= length, left - length, left)


def cosine(x, length, inverse):
    left = reduced(x, length, inverse)
    left = jnp.where(2 * left > length, left - length, left)
    half = left.astype(jnp.float32) * (inverse * math.pi)
    square = half * half
    series = jnp.full_like(square, 1.0 / math.factorial(13))
    for power in (11, 9, 7, 5, 3, 1):
        sign = -1.0 if power % 4 == 3 else 1.0
        series = series * square + sign / math.factorial(power)
    sine = series * half
    return 1.0 - 2.0 * sine * sine


def synthesis(columns, got, wave, points, owner, out, coeffs, swapped, grid, out_sem):
    groups, lanes = got.shape[0], got.shape[3]
    depth = 4 * columns
    count, fields, level_total, segment = grid.shape
    levels = level_total // groups
    block = fields * level_total
    copies = -(-3 * depth // 128) * 128 // depth
    wide = copies * depth
    tiles = segment // 128
    tile_rows = -(-tiles // 8) * 8
    g, w = lax.axis_index("grp"), lax.axis_index("wav")

    x = jnp.concatenate([got[i].reshape(depth, lanes) for i in range(groups)], axis=1)
    even = iota(x.shape, 0) % 2 == 0
    partner = jnp.where(even, pltpu.roll(x, depth - 1, 0), pltpu.roll(x, 1, 0))
    target = iota((count * block, 1), 0)
    inner = lax.rem(target, block)
    level = lax.rem(inner, level_total)
    target = (
        lax.div(level, levels) * lanes
        + lax.div(target, block) * SLOTS
        + lax.div(inner, level_total) * levels
        + lax.rem(level, levels)
    )
    move = iota((count * block, groups * lanes), 1) == target
    move = move.astype(jnp.float32).astype(jnp.bfloat16)
    for values, ref in ((x, coeffs), (partner, swapped)):
        high, low = split(values)
        ref[...] = dot(move, jnp.concatenate([high] * copies, axis=0), ((1,), (1,))) + dot(
            move, jnp.concatenate([low] * copies, axis=0), ((1,), (1,))
        )

    deep = iota((depth, 128), 0)
    deep_wave = jnp.zeros((depth, 128), jnp.int32)
    across = iota((tile_rows, wide), 1) % depth
    across_wave = jnp.zeros((tile_rows, wide), jnp.int32)
    for q in range(depth // 2):
        deep_wave = jnp.where(deep // 2 == q, wave[q], deep_wave)
        across_wave = jnp.where(across // 2 == q, wave[q], across_wave)
    near = deep_wave * iota((depth, 128), 1)
    far = across_wave * (w * segment + 128 * iota((tile_rows, wide), 0))
    weight = jnp.where(across_wave == 0, 1.0, 2.0)
    rest = (iota((block * tiles, wide), 1) // depth) % 2 == 1
    point = iota((block, 128), 1) + w * segment

    def write(p):
        return pltpu.make_async_copy(grid.at[p], out.at[p], out_sem.at[p])

    @pl.loop(0, count, unroll=16)
    def _(p):
        length = points[lax.rem(owner[g * count + p], points.shape[0])]
        quarter = lax.div(length, 4)
        inverse = 1.0 / jnp.full((1, 128), length, jnp.int32).astype(jnp.float32)
        high, low = split(cosine(near + (deep % 2) * quarter, length, inverse))
        basis = jnp.concatenate([high, high, low, low][:copies], axis=0)
        inverse = jnp.concatenate([inverse] * (wide // 128), axis=1)
        turn = weight * cosine(far, length, inverse)
        cross = weight * cosine(far + (1 + 2 * (across % 2)) * quarter, length, inverse)
        start = pl.multiple_of(p * block, 8)
        own, other = coeffs[pl.ds(start, block), :], swapped[pl.ds(start, block), :]
        turned = jnp.concatenate(
            [own * turn[t : t + 1] + other * cross[t : t + 1] for t in range(tiles)], axis=0
        )
        head = turned.astype(jnp.bfloat16).astype(jnp.float32)
        parts = jnp.where(rest, turned - head, head).astype(jnp.bfloat16)
        values = dot(parts, basis)
        for t in range(tiles):
            kept = jnp.where(point + 128 * t < length, values[t * block : (t + 1) * block], 0.0)
            grid[p, :, :, 128 * t : 128 * (t + 1)] = kept.reshape(fields, level_total, 128)
        write(p).start()

    @pl.loop(0, count)
    def _(p):
        write(p).wait()


def body(groups, columns, spectra, legendre, wave_number, cycle_points, cycle_owner):
    fields, levels, waves, _, degrees = spectra.shape
    half = legendre.shape[2]
    count = 2 * half // groups
    lanes = count * SLOTS
    level_total = levels * groups
    segment = (RMAX + 128 * columns - 1) // (128 * columns) * 128
    vmem, smem = pl.BlockSpec(memory_space=pltpu.VMEM), pl.BlockSpec(memory_space=pltpu.SMEM)
    got = pl.pallas_call(
        functools.partial(spread, groups, columns),
        out_shape=jax.ShapeDtypeStruct((groups, columns, 4, lanes), jnp.float32),
        in_specs=[pl.BlockSpec(memory_space=pltpu.HBM)] * 2 + [smem, smem],
        out_specs=vmem,
        scratch_shapes=[
            pltpu.VMEM(spectra.shape, jnp.float32),
            pltpu.VMEM((waves, half, degrees), jnp.float32),
            pltpu.VMEM((waves, 16, degrees), jnp.float32),
            pltpu.VMEM((groups, 4, lanes), jnp.float32),
            pltpu.SemaphoreType.DMA((groups, columns)),
            pltpu.SemaphoreType.DMA((groups, columns)),
            pltpu.SemaphoreType.DMA((2,)),
        ],
        compiler_params=pltpu.CompilerParams(
            collective_id=0, has_side_effects=True, vmem_limit_bytes=VMEM_BYTES
        ),
        name="spread",
    )(spectra, jnp.swapaxes(legendre, 1, 2), wave_number, cycle_owner)
    wide = -(-3 * 4 * columns // 128) * 128
    block = fields * level_total
    return pl.pallas_call(
        functools.partial(synthesis, columns),
        out_shape=jax.ShapeDtypeStruct((count, fields, level_total, segment), jnp.float32),
        in_specs=[vmem, smem, smem, smem],
        out_specs=pl.BlockSpec(memory_space=pl.ANY),
        scratch_shapes=[
            pltpu.VMEM((count * block, wide), jnp.float32),
            pltpu.VMEM((count * block, wide), jnp.float32),
            pltpu.VMEM((count, fields, level_total, segment), jnp.float32),
            pltpu.SemaphoreType.DMA((count,)),
        ],
        compiler_params=pltpu.CompilerParams(vmem_limit_bytes=VMEM_BYTES),
        name="synthesis",
    )(got, wave_number, cycle_points, cycle_owner)


def solution(mesh):
    in_specs = (P(None, "grp", "wav", None, None), P("wav", None, None), P(), P(), P())
    out_specs = P("grp", None, None, "wav")
    groups, columns = mesh.shape["grp"], mesh.shape["wav"]
    return jax.shard_map(
        functools.partial(body, groups, columns),
        mesh=mesh,
        in_specs=in_specs,
        out_specs=out_specs,
        check_vma=False,
    )
```
